32 devices in a mesh: seg: 4 (over y, x), gx: 8 (over z, core).
Axes of the slice: x: 2, y: 2, z: 4, core: 2. Of those that a mesh axis runs over, the one named last changes fastest.
Arguments:
- start_states: float32 [4, 3, 24, 64, 384], P('seg', None, 'gx'), may hold values from -6 to 6
- base_flow: bfloat16 [4, 3, 3, 24, 64, 384], P('seg', None, None, 'gx'), may hold values from -3.5 to 3.5
Outputs:
- residual: float32 [4, 3, 24, 64, 384], P('seg', None, 'gx')
The draws below stay inside these ranges and needn't reach their ends.
All inputs are finite; a program needn't handle non-finite values.
Results may differ from the reference program's by a relative error of at most 0.0015.
Values may be sent and summed in bfloat16 or wider, within the bound.
A program may use at most 128 MiB of HBM per device.

```python
import jax
import jax.numpy as jnp

NY = 64
NZ = 384
STEPS = 3
SEGMENTS = 4
NX = 24


def shard_levels(rng, dims, shards, low, high):
    level, own = 1.0, jax.random.fold_in(rng, 6)
    for position, parts in shards:
        draws = jnp.exp(jax.random.uniform(jax.random.fold_in(own, position), (parts,), jnp.float32, low / len(shards), high / len(shards)))
        level = level * jnp.repeat(draws, dims[position] // parts).reshape([-1 if axis == position else 1 for axis in range(len(dims))])
    return level


def bell_draw(rng, dims, spread, most, pieces=(), kind=jnp.bfloat16):
    level = shard_levels(rng, dims, pieces, -0.22, 0.18) if pieces else 1.0
    values = jax.random.normal(rng, dims, jnp.float32) * spread * level
    return jnp.minimum(jnp.maximum(values, -most), most).astype(kind)


def setup_inputs(seed: int = 0) -> dict:
    streams_of = jax.random.split(jax.random.key(seed), 3)
    start_states = bell_draw(streams_of[0], (SEGMENTS, 3, NX, NY, NZ), 1.0, 6.0, ((0, 4), (2, 8)), jnp.float32)
    base_flow = bell_draw(streams_of[1], (SEGMENTS, STEPS, 3, NX, NY, NZ), 0.6, 3.5, ((0, 4), (3, 8)))
    return dict(start_states=start_states, base_flow=base_flow)


time_step = 0.3
viscosity = 0.45


def advance(q_ext, b_ext):
    centre = q_ext[:, 1:-1]
    base_c = b_ext[:, 1:-1]
    zero_row = jnp.zeros((3, centre.shape[1], 1, centre.shape[3]), jnp.float32)
    q_pad = jnp.concatenate([zero_row, centre, zero_row], axis=2)
    wall_sign = jnp.concatenate([jnp.ones((1, centre.shape[1], 1, centre.shape[3]), jnp.float32), jnp.zeros((2, centre.shape[1], 1, centre.shape[3]), jnp.float32)], axis=0)
    b_pad = jnp.concatenate([-wall_sign, base_c, wall_sign], axis=2)
    q_up = jnp.roll(centre, -1, 3)
    q_down = jnp.roll(centre, 1, 3)
    dq_x = (q_ext[:, 2:] - q_ext[:, :-2]) * 0.5
    dq_y = (q_pad[:, :, 2:] - q_pad[:, :, :-2]) * 0.5
    dq_z = (q_up - q_down) * 0.5
    db_x = (b_ext[:, 2:] - b_ext[:, :-2]) * 0.5
    db_y = (b_pad[:, :, 2:] - b_pad[:, :, :-2]) * 0.5
    db_z = (jnp.roll(base_c, -1, 3) - jnp.roll(base_c, 1, 3)) * 0.5
    lap = q_ext[:, 2:] + q_ext[:, :-2] + q_pad[:, :, 2:] + q_pad[:, :, :-2] + q_up + q_down - 6.0 * centre
    advect = base_c[0:1] * dq_x + base_c[1:2] * dq_y + base_c[2:3] * dq_z
    produce = centre[0:1] * db_x + centre[1:2] * db_y + centre[2:3] * db_z
    return centre + time_step * (viscosity * lap - advect - produce)


def wrapped(field, width):
    return jnp.concatenate([field[:, -width:], field, field[:, :width]], axis=1)


def mirror(field):
    shifted = jnp.roll(field, NX // 2, axis=1)
    flipped = jnp.roll(jnp.flip(shifted, 3), 1, 3)
    sign = jnp.concatenate([jnp.ones((2, 1, 1, 1), jnp.float32), -jnp.ones((1, 1, 1, 1), jnp.float32)], axis=0)
    return flipped * sign


def reference(start_states, base_flow):
    outputs = []
    for segment in range(SEGMENTS):
        state = start_states[segment]
        for step in range(STEPS):
            state = advance(wrapped(state, 1), wrapped(base_flow[segment, step].astype(jnp.float32), 1))
        if segment < SEGMENTS - 1:
            outputs.append(state - start_states[segment + 1])
        else:
            outputs.append(state - mirror(start_states[0]))
    return jnp.stack(outputs)
```

```python
import functools

import jax
import jax.numpy as jnp
from jax import lax
from jax.experimental import pallas as pl
from jax.experimental.pallas import tpu as pltpu
from jax.sharding import PartitionSpec as P

TIME_STEP = 0.3
VISCOSITY = 0.45
HALF = 0.5 * TIME_STEP
DIFFUSE = TIME_STEP * VISCOSITY
MESH = pl.DeviceIdType.MESH
ROWS = 16
PAD_Q = 8
PAD_B = 16
RELAY_AT = 1
F32 = jnp.float32
BF16 = jnp.bfloat16

PLANES = {"Q0": (0, 1), "S0": (1, 1), "G": (2, 2), "U": (4, 1), "H": (5, 2), "L": (7, 2)}
KINDS = tuple(PLANES)


def encode(values):
    square = values * values
    fourth = square * square
    eighth = fourth * fourth
    return jnp.where(values < 0, -eighth, eighth).astype(BF16)


def decode(code):
    code = code.astype(F32)
    size = jnp.sqrt(jnp.sqrt(jnp.sqrt(jnp.abs(code))))
    return jnp.where(code < 0, -size, size)


def kernel(n_seg, n_gx, nl, ny, nz, start_ref, base_ref, out_ref, q, b, hq, hb, sq, nq, ub, gp, enc, rt, ra, rb, tq,
           load_sem, qs_sem, qr_sem, bs_sem, br_sem, shift_sem, a_sem, ar_sem, b_sem, c_sem, cr_sem):
    seg = lax.axis_index("seg")
    gx = lax.axis_index("gx")
    last = n_seg - 1
    left, right = lax.rem(gx + n_gx - 1, n_gx), lax.rem(gx + 1, n_gx)
    across = lax.rem(gx + n_gx // 2, n_gx)
    relays = (0, 1, 2, last)
    quarter = ny // 4
    far = lax.rem(gx, 2)
    near = 1 - far
    inner_rows = pl.ds(PAD_B, ny)

    def edge(s):
        return s * (nl - 1)

    load_q = pltpu.make_async_copy(start_ref.at[0], q.at[0, :, :, pl.ds(PAD_Q, ny), :], load_sem.at[0])
    load_q.start()
    load_b = [
        pltpu.make_async_copy(base_ref.at[0, k], b.at[k, :, :, inner_rows, :], load_sem.at[1 + k]) for k in range(3)
    ]
    for copy in load_b:
        copy.start()

    barrier = pltpu.get_barrier_semaphore()
    for other in (left, right, across):
        pl.semaphore_signal(barrier, inc=1, device_id={"gx": other}, device_id_type=MESH)
    for d in range(1, n_seg):
        pl.semaphore_signal(barrier, inc=1, device_id={"seg": lax.rem(seg + d, n_seg)}, device_id_type=MESH)

    def neighbour(s):
        return {"gx": lax.rem(gx + n_gx - 1 + 2 * s, n_gx)}

    def q_copy(kind, s):
        first, count = PLANES[kind]
        at, i = pl.ds(first, count), KINDS.index(kind)
        return pltpu.make_async_remote_copy(
            src_ref=sq.at[s, at], dst_ref=hq.at[1 - s, at], send_sem=qs_sem.at[i, s], recv_sem=qr_sem.at[i, 1 - s],
            device_id=neighbour(s), device_id_type=MESH)

    def b_copy(k, s):
        return pltpu.make_async_remote_copy(
            src_ref=base_ref.at[0, k, 0, edge(s)], dst_ref=hb.at[1 - s, k, inner_rows],
            send_sem=bs_sem.at[k, s], recv_sem=br_sem.at[k, 1 - s],
            device_id=neighbour(s), device_id_type=MESH)

    shift = pltpu.make_async_remote_copy(
        src_ref=enc, dst_ref=rt, send_sem=shift_sem.at[0], recv_sem=shift_sem.at[1],
        device_id={"seg": lax.rem(seg + n_seg - 1, n_seg)}, device_id_type=MESH)

    def a_copy(j):
        return pltpu.make_async_remote_copy(
            src_ref=enc.at[j], dst_ref=ra, send_sem=a_sem.at[j], recv_sem=ar_sem.at[0],
            device_id={"seg": relays[j]}, device_id_type=MESH)

    def z_copy(source):
        return pltpu.make_async_remote_copy(
            src_ref=source, dst_ref=rb, send_sem=b_sem.at[0], recv_sem=b_sem.at[1],
            device_id={"gx": across}, device_id_type=MESH)

    def c_copy(j):
        return pltpu.make_async_remote_copy(
            src_ref=rb, dst_ref=tq.at[j], send_sem=c_sem.at[0], recv_sem=cr_sem.at[j],
            device_id={"seg": last}, device_id_type=MESH)

    q[:, :, :, 0:PAD_Q, :] = jnp.zeros((2, 3, nl, PAD_Q, nz), F32)
    q[:, :, :, PAD_Q + ny:, :] = jnp.zeros((2, 3, nl, PAD_Q, nz), F32)
    for c in range(3):
        wall = jnp.full((3, nl, PAD_B, nz), 1.0 if c == 0 else 0.0, BF16)
        b[:, c, :, 0:PAD_B, :] = -wall
        b[:, c, :, PAD_B + ny:, :] = wall
    wall = jnp.full((2, PAD_B, nz), 1.0, BF16)
    hb[:, 1, 0:PAD_B, :] = -wall
    hb[:, 1, PAD_B + ny:, :] = wall

    load_q.wait()
    for s in range(2):
        sq[s, 0] = q[0, 0, edge(s), PAD_Q:PAD_Q + ny, :].astype(BF16)
    pl.semaphore_wait(barrier, 3 + n_seg - 1)
    for s in (far, near):
        b_copy(0, s).start()
        q_copy("Q0", s).start()

    def by_rows(chunk):
        def body(r, carry):
            chunk(pl.multiple_of(r * ROWS, ROWS))
            return carry

        lax.fori_loop(0, ny // ROWS, body, 0, unroll=True)

    def sign(s):
        return jnp.where(s == 0, HALF, -HALF).astype(F32)

    def shifted(window, pad):
        size = window.shape[0]
        up = pltpu.roll(window, size - 1, 0)[pad:pad + ROWS]
        down = pltpu.roll(window, 1, 0)[pad:pad + ROWS]
        return up, down

    def slopes(window):
        up, down = shifted(window[PAD_B - 8:PAD_B + ROWS + 8], 8)
        base = window[PAD_B:PAD_B + ROWS]
        return up - down, pltpu.roll(base, nz - 1, 1) - pltpu.roll(base, 1, 1)

    def q_at(k, c, x, at):
        return q[k % 2, c, x, pl.ds(at + PAD_Q, ROWS), :]

    def b_at(k, c, x, at):
        return b[k, c, x, pl.ds(at + PAD_B, ROWS), :].astype(F32)

    def hb_at(s, k, at):
        return hb[s, k, pl.ds(at + PAD_B, ROWS), :].astype(F32)

    def hq_at(s, i, at):
        return hq[s, i, pl.ds(at, ROWS), :].astype(F32)

    def stencil(k, x, at, comps, side=None):
        slot = k % 2
        windows = [b[k, c, x, pl.ds(at, ROWS + 2 * PAD_B), :].astype(F32) for c in range(3)]
        carried = [HALF * window[PAD_B:PAD_B + ROWS] for window in windows]
        ahead = [DIFFUSE - value for value in carried]
        behind = [DIFFUSE + value for value in carried]
        centres = [q_at(k, c, x, at) for c in range(3)]
        pushed = [HALF * value for value in centres]
        if side is not None:
            towards = 2.0 * sign(side) / TIME_STEP
            weight = DIFFUSE - towards * carried[0]
            push = towards * pushed[0]
            inward = x + 1 - 2 * side
        totals = []
        for c in comps:
            window = q[slot, c, x, pl.ds(at, ROWS + 2 * PAD_Q), :]
            centre = centres[c]
            up, down = shifted(window, PAD_Q)
            total = (1.0 - 6.0 * DIFFUSE) * centre
            if side is None:
                total += ahead[0] * q_at(k, c, x + 1, at) - pushed[0] * b_at(k, c, x + 1, at)
                total += behind[0] * q_at(k, c, x - 1, at) + pushed[0] * b_at(k, c, x - 1, at)
            else:
                total += weight * q_at(k, c, inward, at) - push * b_at(k, c, inward, at)
            total += ahead[1] * up + behind[1] * down
            total += ahead[2] * pltpu.roll(centre, nz - 1, 1) + behind[2] * pltpu.roll(centre, 1, 1)
            rise, run = slopes(windows[c])
            total -= pushed[1] * rise
            total -= pushed[2] * run
            totals.append(total)
        return totals

    def inner(k, x):
        def chunk(at):
            for c, total in enumerate(stencil(k, x, at, range(3))):
                if k == 2:
                    out_ref[0, c, x, pl.ds(at, ROWS), :] = total
                else:
                    q[1 - k % 2, c, x, pl.ds(at + PAD_Q, ROWS), :] = total

        by_rows(chunk)

    def first(s):
        x = edge(s)

        def chunk(at):
            totals = stencil(0, x, at, range(3), s)
            for c in range(3):
                q[1, c, x, pl.ds(at + PAD_Q, ROWS), :] = totals[c]
            sq[s, 1, pl.ds(at, ROWS), :] = totals[0].astype(BF16)

        by_rows(chunk)
        q_copy("S0", s).start()
        b_copy(1, s).start()

    def exchange(s):
        x, signed = edge(s), sign(s)
        b_copy(0, 1 - s).wait_recv()
        q_copy("Q0", 1 - s).wait_recv()

        def chunk(at):
            here, inside = pl.ds(at, ROWS), pl.ds(at + PAD_Q, ROWS)
            carried, pushed = signed * hb_at(s, 0, at), hq_at(s, 0, at)
            weight, push = DIFFUSE - carried, signed * pushed
            mine, base = q_at(0, 0, x, at), b_at(0, 0, x, at)
            nq[s, here, :] = weight * mine - push * base
            q[1, 0, x, inside, :] += (DIFFUSE + signed * base) * pushed + mine * carried
            for c in range(1, 3):
                share = weight * q_at(0, c, x, at) - push * b_at(0, c, x, at)
                sq[s, 1 + c, here, :] = share.astype(BF16)

        by_rows(chunk)
        q_copy("G", s).start()

    def ahead_of(s):
        x = edge(s)

        def chunk(at):
            total, = stencil(1, x, at, range(1), s)
            ub[s, pl.ds(at, ROWS), :] = total
            sq[s, 4, pl.ds(at, ROWS), :] = total.astype(BF16)

        by_rows(chunk)
        q_copy("U", s).start()

    def second(s):
        x, signed = edge(s), sign(s)
        b_copy(1, 1 - s).wait_recv()
        q_copy("S0", 1 - s).wait_recv()

        def chunk(at):
            here = pl.ds(at, ROWS)
            theirs = nq[s, here, :] + hq_at(s, 1, at)
            nq[s, here, :] = theirs
            weight, push = DIFFUSE - signed * hb_at(s, 1, at), signed * theirs
            for c in range(1, 3):
                share = weight * q_at(1, c, x, at) - push * b_at(1, c, x, at)
                sq[s, 4 + c, here, :] = share.astype(BF16)

        by_rows(chunk)
        q_copy("H", s).start()

    def prepare(s):
        x, signed = edge(s), sign(s)

        def chunk(at):
            here = pl.ds(at, ROWS)
            theirs = nq[s, here, :]
            window = hb[s, 1, pl.ds(at, ROWS + 2 * PAD_B), :].astype(F32)
            carried = signed * window[PAD_B:PAD_B + ROWS]
            mine, base = q_at(1, 0, x, at), b_at(1, 0, x, at)
            weight = DIFFUSE + signed * base
            ub[s, here, :] += weight * theirs + mine * carried
            shares = [sq[s, 1 + c, here, :].astype(F32) for c in range(1, 3)]
            rise, run = slopes(window)
            kept = (DIFFUSE - carried) * mine - (signed * theirs) * base
            nq[s, here, :] = kept - HALF * (shares[0] * rise + shares[1] * run)
            for c in range(2):
                gp[s, c, here, :] = weight * shares[c]

        by_rows(chunk)

    def third(s):
        x, signed = edge(s), sign(s)
        q_copy("G", 1 - s).wait_recv()

        def add(at):
            here, inside = pl.ds(at, ROWS), pl.ds(at + PAD_Q, ROWS)
            shares = [hq_at(s, 1 + c, at) for c in range(1, 3)]
            rise, run = slopes(b[1, 0, x, pl.ds(at, ROWS + 2 * PAD_B), :].astype(F32))
            q[0, 0, x, inside, :] = ub[s, here, :] - HALF * (shares[0] * rise + shares[1] * run)
            for c in range(1, 3):
                q[1, c, x, inside, :] += shares[c - 1]

        by_rows(add)
        q_copy("U", 1 - s).wait_recv()
        q_copy("H", 1 - s).wait_recv()
        b_copy(2, 1 - s).wait_recv()

        def chunk(at):
            here, inside = pl.ds(at, ROWS), pl.ds(at + PAD_Q, ROWS)
            theirs = nq[s, here, :] + hq_at(s, 4, at)
            nq[s, here, :] = theirs
            weight, push = DIFFUSE - signed * hb_at(s, 2, at), signed * theirs
            for c, total in zip((1, 2), stencil(1, x, at, (1, 2), s)):
                total += gp[s, c - 1, here, :] + hq_at(s, 4 + c, at)
                q[0, c, x, inside, :] = total
                sq[s, 6 + c, here, :] = (weight * total - push * b_at(2, c, x, at)).astype(BF16)

        by_rows(chunk)
        q_copy("L", s).start()

    def final(s):
        x, signed = edge(s), sign(s)

        def chunk(at):
            here = pl.ds(at, ROWS)
            totals = stencil(2, x, at, range(3), s)
            carried = signed * b_at(2, 0, x, at)
            totals[0] += (DIFFUSE + carried) * nq[s, here, :] + (signed * q_at(2, 0, x, at)) * hb_at(s, 2, at)
            for c in range(3):
                out_ref[0, c, x, here, :] = totals[c]

        by_rows(chunk)

    def close(s):
        x = edge(s)
        q_copy("L", 1 - s).wait_recv()

        def chunk(at):
            for c in range(1, 3):
                out_ref[0, c, x, pl.ds(at, ROWS), :] += hq_at(s, 6 + c, at)

        by_rows(chunk)

    def is_relay():
        flag = seg == 0
        for r in relays[1:]:
            flag = flag | (seg == r)
        return flag

    def start_relay():
        @pl.when(seg == 0)
        def _():
            z_copy(enc.at[0]).start()

        @pl.when((seg != 0) & is_relay())
        def _():
            a_copy(0).wait_recv()
            z_copy(ra).start()

    def forward_relay():
        @pl.when(is_relay() & (seg != last))
        def _():
            z_copy(ra).wait_recv()
            for j in range(3):
                @pl.when(seg == relays[j])
                def _():
                    c_copy(j).start()

    def subtract_target():
        @pl.when(seg < last)
        def _():
            shift.wait_recv()
            for j in range(4):
                for c in range(3):
                    out_ref[0, c, :, j * quarter:(j + 1) * quarter, :] -= decode(rt[j, c])

        @pl.when(seg == last)
        def _():
            z_copy(ra).wait_recv()
            for j in range(3):
                c_copy(j).wait_recv()
            row = lax.broadcasted_iota(jnp.int32, (nz, nz), 0)
            column = lax.broadcasted_iota(jnp.int32, (nz, nz), 1)
            flip = jnp.where((row + column == 0) | (row + column == nz), 1.0, 0.0).astype(BF16)
            for j in range(4):
                source = rb if j == 3 else tq.at[j]
                for c in range(3):
                    values = decode(source[c]).reshape(nl * quarter, nz)
                    high = values.astype(BF16)
                    low = (values - high.astype(F32)).astype(BF16)
                    flipped = jnp.dot(high, flip, preferred_element_type=F32)
                    flipped += jnp.dot(low, flip, preferred_element_type=F32)
                    if c == 2:
                        flipped = -flipped
                    out_ref[0, c, :, j * quarter:(j + 1) * quarter, :] -= flipped.reshape(nl, quarter, nz)

    for j in range(4):
        for c in range(3):
            enc[j, c] = encode(q[0, c, :, PAD_Q + j * quarter:PAD_Q + (j + 1) * quarter, :])

    @pl.when(seg == 0)
    def _():
        for j in range(1, 4):
            a_copy(j).start()

    @pl.when(seg > 0)
    def _():
        shift.start()

    load_b[0].wait()
    first(far)
    first(near)
    for x in range(1, nl - 1):
        inner(0, x)
    load_b[1].wait()
    exchange(near)
    exchange(far)
    if RELAY_AT == 0:
        start_relay()
    ahead_of(far)
    ahead_of(near)
    if RELAY_AT == 1:
        start_relay()
    second(near)
    second(far)
    b_copy(2, far).start()
    b_copy(2, near).start()
    if RELAY_AT == 2:
        start_relay()
    prepare(near)
    prepare(far)
    load_b[2].wait()
    third(near)
    third(far)
    for x in range(1, nl - 1):
        inner(1, x)
    forward_relay()
    final(near)
    final(far)
    for x in range(1, nl - 1):
        inner(2, x)
    subtract_target()
    close(near)
    close(far)

    for s in range(2):
        for kind in KINDS:
            q_copy(kind, s).wait_send()
        for k in range(3):
            b_copy(k, s).wait_send()

    @pl.when(seg > 0)
    def _():
        shift.wait_send()

    @pl.when(seg == 0)
    def _():
        for j in range(1, 4):
            a_copy(j).wait_send()

    @pl.when(is_relay())
    def _():
        z_copy(ra).wait_send()

    @pl.when(is_relay() & (seg != last))
    def _():
        c_copy(0).wait_send()


def local(n_seg, n_gx, start_states, base_flow):
    _, _, nl, ny, nz = start_states.shape
    assert base_flow.shape[1] == 3 and nl >= 3
    quarter = ny // 4
    dma = pltpu.SemaphoreType.DMA
    return pl.pallas_call(
        functools.partial(kernel, n_seg, n_gx, nl, ny, nz),
        out_shape=jax.ShapeDtypeStruct(start_states.shape, F32),
        in_specs=[pl.BlockSpec(memory_space=pltpu.HBM)] * 2,
        out_specs=pl.BlockSpec(memory_space=pltpu.VMEM),
        scratch_shapes=[
            pltpu.VMEM((2, 3, nl, ny + 2 * PAD_Q, nz), F32),
            pltpu.VMEM((3, 3, nl, ny + 2 * PAD_B, nz), BF16),
            pltpu.VMEM((2, 9, ny, nz), BF16),
            pltpu.VMEM((2, 3, ny + 2 * PAD_B, nz), BF16),
            pltpu.VMEM((2, 9, ny, nz), BF16),
            pltpu.VMEM((2, ny, nz), F32),
            pltpu.VMEM((2, ny, nz), F32),
            pltpu.VMEM((2, 2, ny, nz), F32),
            pltpu.VMEM((4, 3, nl, quarter, nz), BF16),
            pltpu.VMEM((4, 3, nl, quarter, nz), BF16),
            pltpu.VMEM((3, nl, quarter, nz), BF16),
            pltpu.VMEM((3, nl, quarter, nz), BF16),
            pltpu.VMEM((3, 3, nl, quarter, nz), BF16),
            dma((4,)),
            dma((len(KINDS), 2)), dma((len(KINDS), 2)),
            dma((3, 2)), dma((3, 2)),
            dma((2,)),
            dma((4,)), dma((1,)),
            dma((2,)),
            dma((1,)), dma((3,)),
        ],
        compiler_params=pltpu.CompilerParams(
            collective_id=0, has_side_effects=True, vmem_limit_bytes=44 * 1024 * 1024),
        cost_estimate=pl.CostEstimate(flops=60_000_000, bytes_accessed=4_000_000, transcendentals=0),
    )(pltpu.with_memory_space_constraint(start_states, pltpu.HBM), pltpu.with_memory_space_constraint(base_flow, pltpu.HBM))


def solution(mesh):
    in_specs = (P("seg", None, "gx", None, None), P("seg", None, None, "gx", None, None))
    out_specs = P("seg", None, "gx", None, None)
    body = functools.partial(local, mesh.shape["seg"], mesh.shape["gx"])
    return jax.shard_map(body, mesh=mesh, in_specs=in_specs, out_specs=out_specs, check_vma=False)
```

```python
import functools

import jax
import jax.numpy as jnp
from jax import lax
from jax.experimental import pallas as pl
from jax.experimental.pallas import tpu as pltpu
from jax.sharding import PartitionSpec as P

TIME_STEP = 0.3
VISCOSITY = 0.45
HALF = 0.5 * TIME_STEP
DIFFUSE = TIME_STEP * VISCOSITY
MESH = pl.DeviceIdType.MESH
ROWS = 16
PAD_Q = 8
PAD_B = 16
ACROSS = (0, 1, 1, 2)
FORWARD = (4, 5, 5)
F32 = jnp.float32
BF16 = jnp.bfloat16

PLANES = {"Q0": (0, 1), "S0": (1, 1), "G": (2, 2), "U": (4, 1), "H": (5, 2), "L": (7, 2)}
KINDS = tuple(PLANES)


def encode(values):
    square = values * values
    fourth = square * square
    eighth = fourth * fourth
    return jnp.where(values < 0, -eighth, eighth).astype(BF16)


def decode(code):
    code = code.astype(F32)
    size = jnp.sqrt(jnp.sqrt(jnp.sqrt(jnp.abs(code))))
    return jnp.where(code < 0, -size, size)


def kernel(n_seg, n_gx, nl, ny, nz, start_ref, base_ref, out_ref, q, b, hq, hb, sq, nq, ub, gp, eq, enc, rt, ra, rb, tq,
           load_sem, qs_sem, qr_sem, bs_sem, br_sem, shift_sem, a_sem, ar_sem, b_sem, c_sem, cr_sem):
    seg = lax.axis_index("seg")
    gx = lax.axis_index("gx")
    last = n_seg - 1
    left, right = lax.rem(gx + n_gx - 1, n_gx), lax.rem(gx + 1, n_gx)
    across = lax.rem(gx + n_gx // 2, n_gx)
    relays = (0, 1, 2, last)
    quarter = ny // 4
    far = lax.rem(gx, 2)
    near = 1 - far
    inner_rows = pl.ds(PAD_B, ny)

    def edge(s):
        return s * (nl - 1)

    barrier = pltpu.get_barrier_semaphore()
    for other in (left, right, across):
        pl.semaphore_signal(barrier, inc=1, device_id={"gx": other}, device_id_type=MESH)
    for d in range(1, n_seg):
        pl.semaphore_signal(barrier, inc=1, device_id={"seg": lax.rem(seg + d, n_seg)}, device_id_type=MESH)

    load_edge = [pltpu.make_async_copy(start_ref.at[0, 0, edge(s)], eq.at[s], load_sem.at[4 + s]) for s in range(2)]
    load_q = pltpu.make_async_copy(start_ref.at[0], q.at[0, :, :, pl.ds(PAD_Q, ny), :], load_sem.at[0])
    load_b = [
        pltpu.make_async_copy(base_ref.at[0, k], b.at[k, :, :, inner_rows, :], load_sem.at[1 + k]) for k in range(3)
    ]
    for copy in (*load_edge, load_q, *load_b):
        copy.start()

    def neighbour(s):
        return {"gx": lax.rem(gx + n_gx - 1 + 2 * s, n_gx)}

    def q_copy(kind, s):
        first, count = PLANES[kind]
        at, i = pl.ds(first, count), KINDS.index(kind)
        return pltpu.make_async_remote_copy(
            src_ref=sq.at[s, at], dst_ref=hq.at[1 - s, at], send_sem=qs_sem.at[i, s], recv_sem=qr_sem.at[i, 1 - s],
            device_id=neighbour(s), device_id_type=MESH)

    def b_copy(k, s):
        return pltpu.make_async_remote_copy(
            src_ref=base_ref.at[0, k, 0, edge(s)], dst_ref=hb.at[1 - s, k, inner_rows],
            send_sem=bs_sem.at[k, s], recv_sem=br_sem.at[k, 1 - s],
            device_id=neighbour(s), device_id_type=MESH)

    shift = pltpu.make_async_remote_copy(
        src_ref=enc, dst_ref=rt, send_sem=shift_sem.at[0], recv_sem=shift_sem.at[1],
        device_id={"seg": lax.rem(seg + n_seg - 1, n_seg)}, device_id_type=MESH)

    def a_copy(j):
        return pltpu.make_async_remote_copy(
            src_ref=enc.at[j], dst_ref=ra, send_sem=a_sem.at[j], recv_sem=ar_sem.at[0],
            device_id={"seg": relays[j]}, device_id_type=MESH)

    def z_copy(source):
        return pltpu.make_async_remote_copy(
            src_ref=source, dst_ref=rb, send_sem=b_sem.at[0], recv_sem=b_sem.at[1],
            device_id={"gx": across}, device_id_type=MESH)

    def c_copy(j):
        return pltpu.make_async_remote_copy(
            src_ref=rb, dst_ref=tq.at[j], send_sem=c_sem.at[0], recv_sem=cr_sem.at[j],
            device_id={"seg": last}, device_id_type=MESH)

    wrap = (gx == 0) | (gx == n_gx - 1)

    def greet(s):
        b_copy(0, s).start()
        q_copy("Q0", s).start()
        b_copy(1, s).start()

    for s in range(2):
        load_edge[s].wait()
        sq[s, 0] = eq[s].astype(BF16)
    pl.semaphore_wait(barrier, 3 + n_seg - 1)
    @pl.when(wrap)
    def _():
        greet(far)

    greet(near)

    q[:, :, :, 0:PAD_Q, :] = jnp.zeros((2, 3, nl, PAD_Q, nz), F32)
    q[:, :, :, PAD_Q + ny:, :] = jnp.zeros((2, 3, nl, PAD_Q, nz), F32)
    for c in range(3):
        wall = jnp.full((3, nl, PAD_B, nz), 1.0 if c == 0 else 0.0, BF16)
        b[:, c, :, 0:PAD_B, :] = -wall
        b[:, c, :, PAD_B + ny:, :] = wall
    wall = jnp.full((2, PAD_B, nz), 1.0, BF16)
    hb[:, 1, 0:PAD_B, :] = -wall
    hb[:, 1, PAD_B + ny:, :] = wall

    def by_rows(chunk):
        def body(r, carry):
            chunk(pl.multiple_of(r * ROWS, ROWS))
            return carry

        lax.fori_loop(0, ny // ROWS, body, 0, unroll=True)

    def sign(s):
        return jnp.where(s == 0, HALF, -HALF).astype(F32)

    def shifted(window, pad):
        size = window.shape[0]
        up = pltpu.roll(window, size - 1, 0)[pad:pad + ROWS]
        down = pltpu.roll(window, 1, 0)[pad:pad + ROWS]
        return up, down

    def slopes(window):
        up, down = shifted(window[PAD_B - 8:PAD_B + ROWS + 8], 8)
        base = window[PAD_B:PAD_B + ROWS]
        return up - down, pltpu.roll(base, nz - 1, 1) - pltpu.roll(base, 1, 1)

    def q_at(k, c, x, at):
        return q[k % 2, c, x, pl.ds(at + PAD_Q, ROWS), :]

    def b_at(k, c, x, at):
        return b[k, c, x, pl.ds(at + PAD_B, ROWS), :].astype(F32)

    def hb_at(s, k, at):
        return hb[s, k, pl.ds(at + PAD_B, ROWS), :].astype(F32)

    def hq_at(s, i, at):
        return hq[s, i, pl.ds(at, ROWS), :].astype(F32)

    def stencil(k, x, at, comps, side=None):
        slot = k % 2
        windows = [b[k, c, x, pl.ds(at, ROWS + 2 * PAD_B), :].astype(F32) for c in range(3)]
        carried = [HALF * window[PAD_B:PAD_B + ROWS] for window in windows]
        ahead = [DIFFUSE - value for value in carried]
        behind = [DIFFUSE + value for value in carried]
        centres = [q_at(k, c, x, at) for c in range(3)]
        pushed = [HALF * value for value in centres]
        if side is not None:
            towards = 2.0 * sign(side) / TIME_STEP
            weight = DIFFUSE - towards * carried[0]
            push = towards * pushed[0]
            inward = x + 1 - 2 * side
        totals = []
        for c in comps:
            window = q[slot, c, x, pl.ds(at, ROWS + 2 * PAD_Q), :]
            centre = centres[c]
            up, down = shifted(window, PAD_Q)
            total = (1.0 - 6.0 * DIFFUSE) * centre
            if side is None:
                total += ahead[0] * q_at(k, c, x + 1, at) - pushed[0] * b_at(k, c, x + 1, at)
                total += behind[0] * q_at(k, c, x - 1, at) + pushed[0] * b_at(k, c, x - 1, at)
            else:
                total += weight * q_at(k, c, inward, at) - push * b_at(k, c, inward, at)
            total += ahead[1] * up + behind[1] * down
            total += ahead[2] * pltpu.roll(centre, nz - 1, 1) + behind[2] * pltpu.roll(centre, 1, 1)
            rise, run = slopes(windows[c])
            total -= pushed[1] * rise
            total -= pushed[2] * run
            totals.append(total)
        return totals

    def inner(k, x):
        def chunk(at):
            for c, total in enumerate(stencil(k, x, at, range(3))):
                if k == 2:
                    out_ref[0, c, x, pl.ds(at, ROWS), :] = total
                else:
                    q[1 - k % 2, c, x, pl.ds(at + PAD_Q, ROWS), :] = total

        by_rows(chunk)

    def first(s):
        x = edge(s)

        def chunk(at):
            totals = stencil(0, x, at, range(3), s)
            for c in range(3):
                q[1, c, x, pl.ds(at + PAD_Q, ROWS), :] = totals[c]
            sq[s, 1, pl.ds(at, ROWS), :] = totals[0].astype(BF16)

        by_rows(chunk)

    def exchange(s):
        x, signed = edge(s), sign(s)
        b_copy(0, 1 - s).wait_recv()
        q_copy("Q0", 1 - s).wait_recv()

        def chunk(at):
            here, inside = pl.ds(at, ROWS), pl.ds(at + PAD_Q, ROWS)
            carried, pushed = signed * hb_at(s, 0, at), hq_at(s, 0, at)
            weight, push = DIFFUSE - carried, signed * pushed
            mine, base = q_at(0, 0, x, at), b_at(0, 0, x, at)
            nq[s, here, :] = weight * mine - push * base
            q[1, 0, x, inside, :] += (DIFFUSE + signed * base) * pushed + mine * carried
            for c in range(1, 3):
                share = weight * q_at(0, c, x, at) - push * b_at(0, c, x, at)
                sq[s, 1 + c, here, :] = share.astype(BF16)

        by_rows(chunk)
        q_copy("G", s).start()

    def ahead_of(s):
        x = edge(s)

        def chunk(at):
            total, = stencil(1, x, at, range(1), s)
            ub[s, pl.ds(at, ROWS), :] = total
            sq[s, 4, pl.ds(at, ROWS), :] = total.astype(BF16)

        by_rows(chunk)
        q_copy("U", s).start()

    def second(s):
        x, signed = edge(s), sign(s)
        b_copy(1, 1 - s).wait_recv()
        q_copy("S0", 1 - s).wait_recv()

        def chunk(at):
            here = pl.ds(at, ROWS)
            theirs = nq[s, here, :] + hq_at(s, 1, at)
            nq[s, here, :] = theirs
            weight, push = DIFFUSE - signed * hb_at(s, 1, at), signed * theirs
            for c in range(1, 3):
                share = weight * q_at(1, c, x, at) - push * b_at(1, c, x, at)
                sq[s, 4 + c, here, :] = share.astype(BF16)

        by_rows(chunk)
        q_copy("H", s).start()

    def prepare(s):
        x, signed = edge(s), sign(s)

        def chunk(at):
            here = pl.ds(at, ROWS)
            theirs = nq[s, here, :]
            window = hb[s, 1, pl.ds(at, ROWS + 2 * PAD_B), :].astype(F32)
            carried = signed * window[PAD_B:PAD_B + ROWS]
            mine, base = q_at(1, 0, x, at), b_at(1, 0, x, at)
            weight = DIFFUSE + signed * base
            ub[s, here, :] += weight * theirs + mine * carried
            shares = [sq[s, 1 + c, here, :].astype(F32) for c in range(1, 3)]
            rise, run = slopes(window)
            kept = (DIFFUSE - carried) * mine - (signed * theirs) * base
            nq[s, here, :] = kept - HALF * (shares[0] * rise + shares[1] * run)
            for c in range(2):
                gp[s, c, here, :] = weight * shares[c]

        by_rows(chunk)

    def third(s):
        x, signed = edge(s), sign(s)
        q_copy("G", 1 - s).wait_recv()

        def add(at):
            here, inside = pl.ds(at, ROWS), pl.ds(at + PAD_Q, ROWS)
            shares = [hq_at(s, 1 + c, at) for c in range(1, 3)]
            rise, run = slopes(b[1, 0, x, pl.ds(at, ROWS + 2 * PAD_B), :].astype(F32))
            q[0, 0, x, inside, :] = ub[s, here, :] - HALF * (shares[0] * rise + shares[1] * run)
            for c in range(1, 3):
                q[1, c, x, inside, :] += shares[c - 1]

        by_rows(add)

        def chunk(at):
            for c, total in zip((1, 2), stencil(1, x, at, (1, 2), s)):
                q[0, c, x, pl.ds(at + PAD_Q, ROWS), :] = total + gp[s, c - 1, pl.ds(at, ROWS), :]

        by_rows(chunk)

    def fourth(s):
        x, signed = edge(s), sign(s)
        b_copy(2, 1 - s).wait_recv()
        q_copy("U", 1 - s).wait_recv()
        q_copy("H", 1 - s).wait_recv()

        def chunk(at):
            here, inside = pl.ds(at, ROWS), pl.ds(at + PAD_Q, ROWS)
            theirs = nq[s, here, :] + hq_at(s, 4, at)
            nq[s, here, :] = theirs
            weight, push = DIFFUSE - signed * hb_at(s, 2, at), signed * theirs
            for c in range(1, 3):
                total = q[0, c, x, inside, :] + hq_at(s, 4 + c, at)
                q[0, c, x, inside, :] = total
                sq[s, 6 + c, here, :] = (weight * total - push * b_at(2, c, x, at)).astype(BF16)

        by_rows(chunk)
        q_copy("L", s).start()

    def final(s):
        x, signed = edge(s), sign(s)

        def chunk(at):
            here = pl.ds(at, ROWS)
            totals = stencil(2, x, at, range(3), s)
            carried = signed * b_at(2, 0, x, at)
            totals[0] += (DIFFUSE + carried) * nq[s, here, :] + (signed * q_at(2, 0, x, at)) * hb_at(s, 2, at)
            for c in range(3):
                out_ref[0, c, x, here, :] = totals[c]

        by_rows(chunk)

    def close(s):
        x = edge(s)
        q_copy("L", 1 - s).wait_recv()

        def chunk(at):
            for c in range(1, 3):
                out_ref[0, c, x, pl.ds(at, ROWS), :] += hq_at(s, 6 + c, at)

        by_rows(chunk)

    def is_relay():
        flag = seg == 0
        for r in relays[1:]:
            flag = flag | (seg == r)
        return flag

    def relay(point):
        for j in range(4):
            if ACROSS[j] == point:
                @pl.when(seg == relays[j])
                def _():
                    if j == 0:
                        z_copy(enc.at[0]).start()
                    else:
                        a_copy(j).wait_recv()
                        z_copy(ra).start()
        for j in range(3):
            if FORWARD[j] == point:
                @pl.when(seg == relays[j])
                def _():
                    z_copy(ra).wait_recv()
                    c_copy(j).start()

    def subtract_target():
        @pl.when(seg < last)
        def _():
            shift.wait_recv()
            for j in range(4):
                for c in range(3):
                    out_ref[0, c, :, j * quarter:(j + 1) * quarter, :] -= decode(rt[j, c])

        @pl.when(seg == last)
        def _():
            z_copy(ra).wait_recv()
            for j in range(3):
                c_copy(j).wait_recv()
            row = lax.broadcasted_iota(jnp.int32, (nz, nz), 0)
            column = lax.broadcasted_iota(jnp.int32, (nz, nz), 1)
            flip = jnp.where((row + column == 0) | (row + column == nz), 1.0, 0.0).astype(BF16)
            for j in range(4):
                source = rb if j == 3 else tq.at[j]
                for c in range(3):
                    values = decode(source[c]).reshape(nl * quarter, nz)
                    high = values.astype(BF16)
                    low = (values - high.astype(F32)).astype(BF16)
                    flipped = jnp.dot(high, flip, preferred_element_type=F32)
                    flipped += jnp.dot(low, flip, preferred_element_type=F32)
                    if c == 2:
                        flipped = -flipped
                    out_ref[0, c, :, j * quarter:(j + 1) * quarter, :] -= flipped.reshape(nl, quarter, nz)

    load_q.wait()
    for j in range(4):
        for c in range(3):
            enc[j, c] = encode(q[0, c, :, PAD_Q + j * quarter:PAD_Q + (j + 1) * quarter, :])

    @pl.when(seg == 0)
    def _():
        for j in range(1, 3):
            a_copy(j).start()

    relay(0)
    load_b[0].wait()
    first(far)

    @pl.when(wrap)
    def _():
        q_copy("S0", far).start()
        b_copy(2, far).start()

    first(near)
    q_copy("S0", near).start()
    b_copy(2, near).start()

    @pl.when(seg == 0)
    def _():
        a_copy(3).start()

    @pl.when(seg > 0)
    def _():
        shift.start()

    @pl.when(jnp.logical_not(wrap))
    def _():
        greet(far)
        q_copy("S0", far).start()
        b_copy(2, far).start()

    relay(1)
    for x in range(1, nl - 1):
        inner(0, x)
    load_b[1].wait()
    exchange(near)
    ahead_of(near)
    second(near)
    prepare(near)
    exchange(far)
    relay(2)
    ahead_of(far)
    relay(3)
    second(far)
    relay(4)
    prepare(far)
    load_b[2].wait()
    third(near)
    fourth(near)
    third(far)
    relay(5)
    fourth(far)
    relay(6)
    for x in range(1, nl - 1):
        inner(1, x)
    relay(7)
    final(near)
    final(far)
    for x in range(1, nl - 1):
        inner(2, x)
    relay(8)
    subtract_target()
    close(near)
    close(far)

    for s in range(2):
        for kind in KINDS:
            q_copy(kind, s).wait_send()
        for k in range(3):
            b_copy(k, s).wait_send()

    @pl.when(seg > 0)
    def _():
        shift.wait_send()

    @pl.when(seg == 0)
    def _():
        for j in range(1, 4):
            a_copy(j).wait_send()

    @pl.when(is_relay())
    def _():
        z_copy(ra).wait_send()

    @pl.when(is_relay() & (seg != last))
    def _():
        c_copy(0).wait_send()


def local(n_seg, n_gx, start_states, base_flow):
    _, _, nl, ny, nz = start_states.shape
    assert base_flow.shape[1] == 3 and nl >= 3
    quarter = ny // 4
    dma = pltpu.SemaphoreType.DMA
    return pl.pallas_call(
        functools.partial(kernel, n_seg, n_gx, nl, ny, nz),
        out_shape=jax.ShapeDtypeStruct(start_states.shape, F32),
        in_specs=[pl.BlockSpec(memory_space=pltpu.HBM)] * 2,
        out_specs=pl.BlockSpec(memory_space=pltpu.VMEM),
        scratch_shapes=[
            pltpu.VMEM((2, 3, nl, ny + 2 * PAD_Q, nz), F32),
            pltpu.VMEM((3, 3, nl, ny + 2 * PAD_B, nz), BF16),
            pltpu.VMEM((2, 9, ny, nz), BF16),
            pltpu.VMEM((2, 3, ny + 2 * PAD_B, nz), BF16),
            pltpu.VMEM((2, 9, ny, nz), BF16),
            pltpu.VMEM((2, ny, nz), F32),
            pltpu.VMEM((2, ny, nz), F32),
            pltpu.VMEM((2, 2, ny, nz), F32),
            pltpu.VMEM((2, ny, nz), F32),
            pltpu.VMEM((4, 3, nl, quarter, nz), BF16),
            pltpu.VMEM((4, 3, nl, quarter, nz), BF16),
            pltpu.VMEM((3, nl, quarter, nz), BF16),
            pltpu.VMEM((3, nl, quarter, nz), BF16),
            pltpu.VMEM((3, 3, nl, quarter, nz), BF16),
            dma((6,)),
            dma((len(KINDS), 2)), dma((len(KINDS), 2)),
            dma((3, 2)), dma((3, 2)),
            dma((2,)),
            dma((4,)), dma((1,)),
            dma((2,)),
            dma((1,)), dma((3,)),
        ],
        compiler_params=pltpu.CompilerParams(
            collective_id=0, has_side_effects=True, vmem_limit_bytes=44 * 1024 * 1024),
        cost_estimate=pl.CostEstimate(flops=60_000_000, bytes_accessed=4_000_000, transcendentals=0),
    )(pltpu.with_memory_space_constraint(start_states, pltpu.HBM), pltpu.with_memory_space_constraint(base_flow, pltpu.HBM))


def solution(mesh):
    in_specs = (P("seg", None, "gx", None, None), P("seg", None, None, "gx", None, None))
    out_specs = P("seg", None, "gx", None, None)
    body = functools.partial(local, mesh.shape["seg"], mesh.shape["gx"])
    return jax.shard_map(body, mesh=mesh, in_specs=in_specs, out_specs=out_specs, check_vma=False)
```

```python
import functools

import jax
import jax.numpy as jnp
from jax import lax
from jax.experimental import pallas as pl
from jax.experimental.pallas import tpu as pltpu
from jax.sharding import PartitionSpec as P

TIME_STEP = 0.3
VISCOSITY = 0.45
HALF = 0.5 * TIME_STEP
DIFFUSE = TIME_STEP * VISCOSITY
MESH = pl.DeviceIdType.MESH
ROWS = 16
PAD_Q = 8
PAD_B = 16
ACROSS = (0, 4, 4, 4)
FORWARD = 4
F32 = jnp.float32
BF16 = jnp.bfloat16

PLANES = {"Q0": (0, 1), "S0": (1, 1), "G": (2, 2), "U": (4, 1), "H": (5, 2), "L": (7, 2)}
KINDS = tuple(PLANES)


def encode(values):
    square = values * values
    fourth = square * square
    eighth = fourth * fourth
    return jnp.where(values < 0, -eighth, eighth).astype(BF16)


def decode(code):
    code = code.astype(F32)
    size = jnp.sqrt(jnp.sqrt(jnp.sqrt(jnp.abs(code))))
    return jnp.where(code < 0, -size, size)


def kernel(n_seg, n_gx, nl, ny, nz, start_ref, base_ref, out_ref, q, b, hq, hb, sq, nq, ub, gp, eq, enc, rt, ra, rb, tq,
           load_sem, qs_sem, qr_sem, bs_sem, br_sem, shift_sem, a_sem, ar_sem, z_sem, zr_sem, y_sem, c_sem):
    seg = lax.axis_index("seg")
    gx = lax.axis_index("gx")
    last = n_seg - 1
    left, right = lax.rem(gx + n_gx - 1, n_gx), lax.rem(gx + 1, n_gx)
    across = lax.rem(gx + n_gx // 2, n_gx)
    relays = (0, 1, 2, last)
    quarter = ny // 4
    far = lax.rem(gx, 2)
    near = 1 - far
    inner_rows = pl.ds(PAD_B, ny)

    def is_relay():
        flag = seg == 0
        for r in relays[1:]:
            flag = flag | (seg == r)
        return flag

    def edge(s):
        return s * (nl - 1)

    barrier = pltpu.get_barrier_semaphore()
    for other in (left, right, across):
        pl.semaphore_signal(barrier, inc=1, device_id={"gx": other}, device_id_type=MESH)
    for d in range(1, n_seg):
        pl.semaphore_signal(barrier, inc=1, device_id={"seg": lax.rem(seg + d, n_seg)}, device_id_type=MESH)
    for r in relays[1:3]:
        @pl.when(seg == r)
        def _():
            pl.semaphore_signal(barrier, inc=1, device_id={"seg": last, "gx": across}, device_id_type=MESH)

        @pl.when(seg == last)
        def _():
            pl.semaphore_signal(barrier, inc=1, device_id={"seg": r, "gx": across}, device_id_type=MESH)

    load_edge = [pltpu.make_async_copy(start_ref.at[0, 0, edge(s)], eq.at[s], load_sem.at[4 + s]) for s in range(2)]
    load_q = pltpu.make_async_copy(start_ref.at[0], q.at[0, :, :, pl.ds(PAD_Q, ny), :], load_sem.at[0])
    load_b = [
        pltpu.make_async_copy(base_ref.at[0, k], b.at[k, :, :, inner_rows, :], load_sem.at[1 + k]) for k in range(3)
    ]
    for copy in (*load_edge, load_q, *load_b):
        copy.start()

    def neighbour(s):
        return {"gx": lax.rem(gx + n_gx - 1 + 2 * s, n_gx)}

    def q_copy(kind, s):
        first, count = PLANES[kind]
        at, i = pl.ds(first, count), KINDS.index(kind)
        return pltpu.make_async_remote_copy(
            src_ref=sq.at[s, at], dst_ref=hq.at[1 - s, at], send_sem=qs_sem.at[i, s], recv_sem=qr_sem.at[i, 1 - s],
            device_id=neighbour(s), device_id_type=MESH)

    def b_copy(k, s):
        return pltpu.make_async_remote_copy(
            src_ref=base_ref.at[0, k, 0, edge(s)], dst_ref=hb.at[1 - s, k, inner_rows],
            send_sem=bs_sem.at[k, s], recv_sem=br_sem.at[k, 1 - s],
            device_id=neighbour(s), device_id_type=MESH)

    shift = pltpu.make_async_remote_copy(
        src_ref=enc, dst_ref=rt, send_sem=shift_sem.at[0], recv_sem=shift_sem.at[1],
        device_id={"seg": lax.rem(seg + n_seg - 1, n_seg)}, device_id_type=MESH)

    def a_copy(j):
        return pltpu.make_async_remote_copy(
            src_ref=enc.at[j], dst_ref=ra, send_sem=a_sem.at[j], recv_sem=ar_sem.at[0],
            device_id={"seg": relays[j]}, device_id_type=MESH)

    def z_copy(j, source):
        return pltpu.make_async_remote_copy(
            src_ref=source, dst_ref=tq.at[j], send_sem=z_sem.at[0], recv_sem=zr_sem.at[j],
            device_id={"seg": last, "gx": across}, device_id_type=MESH)

    def y_copy():
        return pltpu.make_async_remote_copy(
            src_ref=enc.at[0], dst_ref=rb, send_sem=y_sem.at[0], recv_sem=y_sem.at[1],
            device_id={"gx": across}, device_id_type=MESH)

    def c_copy():
        return pltpu.make_async_remote_copy(
            src_ref=rb, dst_ref=tq.at[0], send_sem=c_sem.at[0], recv_sem=zr_sem.at[0],
            device_id={"seg": last}, device_id_type=MESH)

    early = (gx == 0) | (gx == n_gx - 1) | (gx == n_gx // 2) | (gx == n_gx // 2 - 1)

    def greet(s):
        b_copy(0, s).start()
        q_copy("Q0", s).start()
        b_copy(1, s).start()

    for s in range(2):
        load_edge[s].wait()
        sq[s, 0] = eq[s].astype(BF16)
    met = jnp.where(seg == last, 2, jnp.where(is_relay() & (seg > 0), 1, 0))
    pl.semaphore_wait(barrier, 3 + n_seg - 1 + met)
    @pl.when(early)
    def _():
        greet(far)

    greet(near)

    q[:, :, :, 0:PAD_Q, :] = jnp.zeros((2, 3, nl, PAD_Q, nz), F32)
    q[:, :, :, PAD_Q + ny:, :] = jnp.zeros((2, 3, nl, PAD_Q, nz), F32)
    for c in range(3):
        wall = jnp.full((3, nl, PAD_B, nz), 1.0 if c == 0 else 0.0, BF16)
        b[:, c, :, 0:PAD_B, :] = -wall
        b[:, c, :, PAD_B + ny:, :] = wall
    wall = jnp.full((2, PAD_B, nz), 1.0, BF16)
    hb[:, 1, 0:PAD_B, :] = -wall
    hb[:, 1, PAD_B + ny:, :] = wall

    def by_rows(chunk):
        def body(r, carry):
            chunk(pl.multiple_of(r * ROWS, ROWS))
            return carry

        lax.fori_loop(0, ny // ROWS, body, 0, unroll=True)

    def sign(s):
        return jnp.where(s == 0, HALF, -HALF).astype(F32)

    def shifted(window, pad):
        size = window.shape[0]
        up = pltpu.roll(window, size - 1, 0)[pad:pad + ROWS]
        down = pltpu.roll(window, 1, 0)[pad:pad + ROWS]
        return up, down

    def slopes(window):
        up, down = shifted(window[PAD_B - 8:PAD_B + ROWS + 8], 8)
        base = window[PAD_B:PAD_B + ROWS]
        return up - down, pltpu.roll(base, nz - 1, 1) - pltpu.roll(base, 1, 1)

    def q_at(k, c, x, at):
        return q[k % 2, c, x, pl.ds(at + PAD_Q, ROWS), :]

    def b_at(k, c, x, at):
        return b[k, c, x, pl.ds(at + PAD_B, ROWS), :].astype(F32)

    def hb_at(s, k, at):
        return hb[s, k, pl.ds(at + PAD_B, ROWS), :].astype(F32)

    def hq_at(s, i, at):
        return hq[s, i, pl.ds(at, ROWS), :].astype(F32)

    def stencil(k, x, at, comps, side=None):
        slot = k % 2
        windows = [b[k, c, x, pl.ds(at, ROWS + 2 * PAD_B), :].astype(F32) for c in range(3)]
        carried = [HALF * window[PAD_B:PAD_B + ROWS] for window in windows]
        ahead = [DIFFUSE - value for value in carried]
        behind = [DIFFUSE + value for value in carried]
        centres = [q_at(k, c, x, at) for c in range(3)]
        pushed = [HALF * value for value in centres]
        if side is not None:
            towards = 2.0 * sign(side) / TIME_STEP
            weight = DIFFUSE - towards * carried[0]
            push = towards * pushed[0]
            inward = x + 1 - 2 * side
        totals = []
        for c in comps:
            window = q[slot, c, x, pl.ds(at, ROWS + 2 * PAD_Q), :]
            centre = centres[c]
            up, down = shifted(window, PAD_Q)
            total = (1.0 - 6.0 * DIFFUSE) * centre
            if side is None:
                total += ahead[0] * q_at(k, c, x + 1, at) - pushed[0] * b_at(k, c, x + 1, at)
                total += behind[0] * q_at(k, c, x - 1, at) + pushed[0] * b_at(k, c, x - 1, at)
            else:
                total += weight * q_at(k, c, inward, at) - push * b_at(k, c, inward, at)
            total += ahead[1] * up + behind[1] * down
            total += ahead[2] * pltpu.roll(centre, nz - 1, 1) + behind[2] * pltpu.roll(centre, 1, 1)
            rise, run = slopes(windows[c])
            total -= pushed[1] * rise
            total -= pushed[2] * run
            totals.append(total)
        return totals

    def inner(k, x):
        def chunk(at):
            for c, total in enumerate(stencil(k, x, at, range(3))):
                if k == 2:
                    out_ref[0, c, x, pl.ds(at, ROWS), :] = total
                else:
                    q[1 - k % 2, c, x, pl.ds(at + PAD_Q, ROWS), :] = total

        by_rows(chunk)

    def first(s):
        x = edge(s)

        def chunk(at):
            totals = stencil(0, x, at, range(3), s)
            for c in range(3):
                q[1, c, x, pl.ds(at + PAD_Q, ROWS), :] = totals[c]
            sq[s, 1, pl.ds(at, ROWS), :] = totals[0].astype(BF16)

        by_rows(chunk)

    def exchange(s):
        x, signed = edge(s), sign(s)
        b_copy(0, 1 - s).wait_recv()
        q_copy("Q0", 1 - s).wait_recv()

        def chunk(at):
            here, inside = pl.ds(at, ROWS), pl.ds(at + PAD_Q, ROWS)
            carried, pushed = signed * hb_at(s, 0, at), hq_at(s, 0, at)
            weight, push = DIFFUSE - carried, signed * pushed
            mine, base = q_at(0, 0, x, at), b_at(0, 0, x, at)
            nq[s, here, :] = weight * mine - push * base
            q[1, 0, x, inside, :] += (DIFFUSE + signed * base) * pushed + mine * carried
            for c in range(1, 3):
                share = weight * q_at(0, c, x, at) - push * b_at(0, c, x, at)
                sq[s, 1 + c, here, :] = share.astype(BF16)

        by_rows(chunk)
        q_copy("G", s).start()

    def ahead_of(s):
        x = edge(s)

        def chunk(at):
            total, = stencil(1, x, at, range(1), s)
            ub[s, pl.ds(at, ROWS), :] = total
            sq[s, 4, pl.ds(at, ROWS), :] = total.astype(BF16)

        by_rows(chunk)
        q_copy("U", s).start()

    def second(s):
        x, signed = edge(s), sign(s)
        b_copy(1, 1 - s).wait_recv()
        q_copy("S0", 1 - s).wait_recv()

        def chunk(at):
            here = pl.ds(at, ROWS)
            theirs = nq[s, here, :] + hq_at(s, 1, at)
            nq[s, here, :] = theirs
            weight, push = DIFFUSE - signed * hb_at(s, 1, at), signed * theirs
            for c in range(1, 3):
                share = weight * q_at(1, c, x, at) - push * b_at(1, c, x, at)
                sq[s, 4 + c, here, :] = share.astype(BF16)

        by_rows(chunk)
        q_copy("H", s).start()

    def prepare(s):
        x, signed = edge(s), sign(s)

        def chunk(at):
            here = pl.ds(at, ROWS)
            theirs = nq[s, here, :]
            window = hb[s, 1, pl.ds(at, ROWS + 2 * PAD_B), :].astype(F32)
            carried = signed * window[PAD_B:PAD_B + ROWS]
            mine, base = q_at(1, 0, x, at), b_at(1, 0, x, at)
            weight = DIFFUSE + signed * base
            ub[s, here, :] += weight * theirs + mine * carried
            shares = [sq[s, 1 + c, here, :].astype(F32) for c in range(1, 3)]
            rise, run = slopes(window)
            kept = (DIFFUSE - carried) * mine - (signed * theirs) * base
            nq[s, here, :] = kept - HALF * (shares[0] * rise + shares[1] * run)
            for c in range(2):
                gp[s, c, here, :] = weight * shares[c]

        by_rows(chunk)

    def third(s):
        x, signed = edge(s), sign(s)
        q_copy("G", 1 - s).wait_recv()

        def add(at):
            here, inside = pl.ds(at, ROWS), pl.ds(at + PAD_Q, ROWS)
            shares = [hq_at(s, 1 + c, at) for c in range(1, 3)]
            rise, run = slopes(b[1, 0, x, pl.ds(at, ROWS + 2 * PAD_B), :].astype(F32))
            q[0, 0, x, inside, :] = ub[s, here, :] - HALF * (shares[0] * rise + shares[1] * run)
            for c in range(1, 3):
                q[1, c, x, inside, :] += shares[c - 1]

        by_rows(add)

        def chunk(at):
            for c, total in zip((1, 2), stencil(1, x, at, (1, 2), s)):
                q[0, c, x, pl.ds(at + PAD_Q, ROWS), :] = total + gp[s, c - 1, pl.ds(at, ROWS), :]

        by_rows(chunk)

    def fourth(s):
        x, signed = edge(s), sign(s)
        b_copy(2, 1 - s).wait_recv()
        q_copy("U", 1 - s).wait_recv()
        q_copy("H", 1 - s).wait_recv()

        def chunk(at):
            here, inside = pl.ds(at, ROWS), pl.ds(at + PAD_Q, ROWS)
            theirs = nq[s, here, :] + hq_at(s, 4, at)
            nq[s, here, :] = theirs
            weight, push = DIFFUSE - signed * hb_at(s, 2, at), signed * theirs
            for c in range(1, 3):
                total = q[0, c, x, inside, :] + hq_at(s, 4 + c, at)
                q[0, c, x, inside, :] = total
                sq[s, 6 + c, here, :] = (weight * total - push * b_at(2, c, x, at)).astype(BF16)

        by_rows(chunk)
        q_copy("L", s).start()

    def final(s):
        x, signed = edge(s), sign(s)

        def chunk(at):
            here = pl.ds(at, ROWS)
            totals = stencil(2, x, at, range(3), s)
            carried = signed * b_at(2, 0, x, at)
            totals[0] += (DIFFUSE + carried) * nq[s, here, :] + (signed * q_at(2, 0, x, at)) * hb_at(s, 2, at)
            for c in range(3):
                out_ref[0, c, x, here, :] = totals[c]

        by_rows(chunk)

    def close(s):
        x = edge(s)
        q_copy("L", 1 - s).wait_recv()

        def chunk(at):
            for c in range(1, 3):
                out_ref[0, c, x, pl.ds(at, ROWS), :] += hq_at(s, 6 + c, at)

        by_rows(chunk)

    def relay(point):
        for j in range(4):
            if ACROSS[j] == point:
                @pl.when(seg == relays[j])
                def _():
                    if j == 0:
                        y_copy().start()
                    else:
                        a_copy(j).wait_recv()
                        z_copy(j, ra).start()
        if FORWARD == point:
            @pl.when(seg == 0)
            def _():
                y_copy().wait_recv()
                c_copy().start()

    def subtract_target():
        @pl.when(seg < last)
        def _():
            shift.wait_recv()
            for j in range(4):
                for c in range(3):
                    out_ref[0, c, :, j * quarter:(j + 1) * quarter, :] -= decode(rt[j, c])

        @pl.when(seg == last)
        def _():
            row = lax.broadcasted_iota(jnp.int32, (nz, nz), 0)
            column = lax.broadcasted_iota(jnp.int32, (nz, nz), 1)
            flip = jnp.where((row + column == 0) | (row + column == nz), 1.0, 0.0).astype(BF16)
            for j in range(4):
                z_copy(j, ra).wait_recv()
                for c in range(3):
                    values = decode(tq[j, c]).reshape(nl * quarter, nz)
                    high = values.astype(BF16)
                    low = (values - high.astype(F32)).astype(BF16)
                    flipped = jnp.dot(high, flip, preferred_element_type=F32)
                    flipped += jnp.dot(low, flip, preferred_element_type=F32)
                    if c == 2:
                        flipped = -flipped
                    out_ref[0, c, :, j * quarter:(j + 1) * quarter, :] -= flipped.reshape(nl, quarter, nz)

    load_q.wait()
    for j in range(4):
        for c in range(3):
            enc[j, c] = encode(q[0, c, :, PAD_Q + j * quarter:PAD_Q + (j + 1) * quarter, :])

    @pl.when(seg == 0)
    def _():
        for j in range(1, 3):
            a_copy(j).start()

    relay(0)
    load_b[0].wait()
    first(far)

    @pl.when(early)
    def _():
        q_copy("S0", far).start()
        b_copy(2, far).start()

    first(near)
    q_copy("S0", near).start()
    b_copy(2, near).start()

    @pl.when(seg == 0)
    def _():
        a_copy(3).start()

    @pl.when(seg > 0)
    def _():
        shift.start()

    @pl.when(jnp.logical_not(early))
    def _():
        greet(far)
        q_copy("S0", far).start()
        b_copy(2, far).start()

    relay(1)
    for x in range(1, nl - 1):
        inner(0, x)
    load_b[1].wait()
    exchange(near)
    ahead_of(near)
    second(near)
    prepare(near)
    exchange(far)
    relay(2)
    ahead_of(far)
    relay(3)
    second(far)
    relay(4)
    prepare(far)
    load_b[2].wait()
    third(near)
    fourth(near)
    third(far)
    relay(5)
    fourth(far)
    relay(6)
    for x in range(1, nl - 1):
        inner(1, x)
    relay(7)
    final(near)
    final(far)
    for x in range(1, nl - 1):
        inner(2, x)
    relay(8)
    subtract_target()
    close(near)
    close(far)

    for s in range(2):
        for kind in KINDS:
            q_copy(kind, s).wait_send()
        for k in range(3):
            b_copy(k, s).wait_send()

    @pl.when(seg > 0)
    def _():
        shift.wait_send()

    @pl.when(seg == 0)
    def _():
        for j in range(1, 4):
            a_copy(j).wait_send()

    @pl.when(seg == 0)
    def _():
        y_copy().wait_send()
        c_copy().wait_send()

    @pl.when(is_relay() & (seg > 0))
    def _():
        z_copy(1, ra).wait_send()


def local(n_seg, n_gx, start_states, base_flow):
    _, _, nl, ny, nz = start_states.shape
    assert base_flow.shape[1] == 3 and nl >= 3
    quarter = ny // 4
    dma = pltpu.SemaphoreType.DMA
    return pl.pallas_call(
        functools.partial(kernel, n_seg, n_gx, nl, ny, nz),
        out_shape=jax.ShapeDtypeStruct(start_states.shape, F32),
        in_specs=[pl.BlockSpec(memory_space=pltpu.HBM)] * 2,
        out_specs=pl.BlockSpec(memory_space=pltpu.VMEM),
        scratch_shapes=[
            pltpu.VMEM((2, 3, nl, ny + 2 * PAD_Q, nz), F32),
            pltpu.VMEM((3, 3, nl, ny + 2 * PAD_B, nz), BF16),
            pltpu.VMEM((2, 9, ny, nz), BF16),
            pltpu.VMEM((2, 3, ny + 2 * PAD_B, nz), BF16),
            pltpu.VMEM((2, 9, ny, nz), BF16),
            pltpu.VMEM((2, ny, nz), F32),
            pltpu.VMEM((2, ny, nz), F32),
            pltpu.VMEM((2, 2, ny, nz), F32),
            pltpu.VMEM((2, ny, nz), F32),
            pltpu.VMEM((4, 3, nl, quarter, nz), BF16),
            pltpu.VMEM((4, 3, nl, quarter, nz), BF16),
            pltpu.VMEM((3, nl, quarter, nz), BF16),
            pltpu.VMEM((3, nl, quarter, nz), BF16),
            pltpu.VMEM((4, 3, nl, quarter, nz), BF16),
            dma((6,)),
            dma((len(KINDS), 2)), dma((len(KINDS), 2)),
            dma((3, 2)), dma((3, 2)),
            dma((2,)),
            dma((4,)), dma((1,)),
            dma((1,)), dma((4,)),
            dma((2,)), dma((1,)),
        ],
        compiler_params=pltpu.CompilerParams(
            collective_id=0, has_side_effects=True, vmem_limit_bytes=44 * 1024 * 1024),
        cost_estimate=pl.CostEstimate(flops=60_000_000, bytes_accessed=4_000_000, transcendentals=0),
    )(pltpu.with_memory_space_constraint(start_states, pltpu.HBM), pltpu.with_memory_space_constraint(base_flow, pltpu.HBM))


def solution(mesh):
    in_specs = (P("seg", None, "gx", None, None), P("seg", None, None, "gx", None, None))
    out_specs = P("seg", None, "gx", None, None)
    body = functools.partial(local, mesh.shape["seg"], mesh.shape["gx"])
    return jax.shard_map(body, mesh=mesh, in_specs=in_specs, out_specs=out_specs, check_vma=False)
```
